32 devices in a mesh: dp: 2 (over x), row: 4 (over y, core), col: 4 (over z).
Axes of the slice: x: 2, y: 2, z: 4, core: 2. Of those that a mesh axis runs over, the one named last changes fastest.
Arguments:
- frames: bfloat16 [4, 1500, 768], P('dp', 'col'), may hold values from -34 to 34
- ln1_gain: float32 [768], P('row'), may hold values from 0.25 to 1.75
- ln1_bias: float32 [768], P('row'), may hold values from -1 to 1
- w_query: bfloat16 [768, 768], P('row', 'col'), may hold values from -0.21875 to 0.21875
- b_query: float32 [768], replicated, may hold values from -1.5 to 1.5
- w_key: bfloat16 [768, 768], P('row', 'col'), may hold values from -0.21875 to 0.21875
- w_value: bfloat16 [768, 768], P('row', 'col'), may hold values from -0.21875 to 0.21875
- b_value: float32 [768], replicated, may hold values from -0.25 to 0.25
- w_out: bfloat16 [768, 768], P('col', 'row'), may hold values from -2 to 2
- b_out: float32 [768], P('row'), may hold values from -1.5 to 1.5
- ln2_gain: float32 [768], P('row'), may hold values from 0.25 to 1.75
- ln2_bias: float32 [768], P('row'), may hold values from -1 to 1
- w_fc1: bfloat16 [768, 3072], P('row', 'col'), may hold values from -0.21875 to 0.21875
- b_fc1: float32 [3072], replicated, may hold values from -1.5 to 1.5
- w_fc2: bfloat16 [768, 3072], P('row', 'col'), may hold values from -0.109375 to 0.109375
- b_fc2: float32 [768], P('row'), may hold values from -1.5 to 1.5
- cotangent: bfloat16 [4, 1500, 768], P('dp', 'col'), may hold values from -6 to 6
Outputs:
- block_out: bfloat16 [4, 1500, 768], P('dp', 'col')
- grad_frames: bfloat16 [4, 1500, 768], P('dp', 'col')
- grad_ln1_gain: float32 [768], P('row')
- grad_ln1_bias: float32 [768], P('row')
- grad_w_query: float32 [768, 768], P('row', 'col')
- grad_b_query: float32 [768], P('col')
- grad_w_key: float32 [768, 768], P('row', 'col')
- grad_w_value: float32 [768, 768], P('row', 'col')
- grad_b_value: float32 [768], P('col')
- grad_w_out: float32 [768, 768], P('col', 'row')
- grad_b_out: float32 [768], P('row')
- grad_ln2_gain: float32 [768], P('row')
- grad_ln2_bias: float32 [768], P('row')
- grad_w_fc1: float32 [768, 3072], P('row', 'col')
- grad_b_fc1: float32 [3072], P('col')
- grad_w_fc2: float32 [768, 3072], P('row', 'col')
- grad_b_fc2: float32 [768], P('row')
The draws below stay inside these ranges and needn't reach their ends.
All inputs are finite; a program needn't handle non-finite values.
Results may differ from the reference program's by a relative error of at most 0.025.
Values may be sent and summed in bfloat16 or wider, within the bound.
A program may use at most 128 MiB of HBM per device.

```python
import math
import jax
import jax.numpy as jnp
from jax import lax

HEADS = 12
HEAD = 64
D = 768
FF = 3072
SEQ = 1500
CLIPS = 4


def draw_frames(key, part):
    key = jax.random.fold_in(key, 7)
    key_noise, key_rough, key_rows = jax.random.split(key, 3)
    position_ramp = jnp.arange(D, dtype=jnp.float32) / (D - 1)
    roughness = jax.random.uniform(key_rough, (D,), jnp.float32, 0.75, 1.33)
    columns = 0.4 * jnp.exp(position_ramp * math.log(6.25)) * roughness
    row_scale = jnp.exp(jax.random.uniform(key_rows, (CLIPS, SEQ, 1), jnp.float32, math.log(0.4), math.log(2.5)))
    noise_draw = jnp.clip(jax.random.normal(key_noise, (CLIPS, SEQ, D), jnp.float32), -4.0, 4.0)
    return (noise_draw * columns * row_scale).astype(jnp.bfloat16)


def level_of(stream_key, extent, cuts, least, high):
    def one(dim, blocks):
        draws = jax.random.uniform(jax.random.fold_in(jax.random.fold_in(stream_key, 6), dim), (blocks,), jnp.float32, least / len(cuts), high / len(cuts))
        return jnp.repeat(jnp.exp(draws), extent[dim] // blocks).reshape((-1,) + (1,) * (len(extent) - dim - 1))

    level = one(*cuts[0])
    for cut in cuts[1:]:
        level = level * one(*cut)
    return level


def gaussian(own_key, extent, scale, reach, shards=(), held_as=jnp.bfloat16):
    values = jax.random.normal(own_key, extent, jnp.float32) * scale
    if len(shards) > 0:
        values = level_of(own_key, extent, shards, -0.22, 0.18) * values
    return jnp.clip(values, min=-reach, max=reach).astype(held_as)


def setup_inputs(seed: int = 0) -> dict:
    arg_keys = jax.random.split(jax.random.key(seed), 18)
    frames = draw_frames(jax.random.fold_in(arg_keys[17], 71), 0)
    ln1_gain = jnp.clip(1.0 + 0.15 * jax.random.normal(arg_keys[1], (D,), jnp.float32), 0.25, 1.75)
    ln1_bias = gaussian(arg_keys[2], (D,), 0.2, 1.0, ((0, 4),), jnp.float32)
    w_query = gaussian(arg_keys[3], (D, D), D ** -0.5, 0.21875, ((0, 4), (1, 4)))
    b_query = gaussian(arg_keys[4], (D,), 0.3, 1.5, (), jnp.float32)
    w_key = gaussian(arg_keys[5], (D, D), D ** -0.5, 0.21875, ((0, 4), (1, 4)))
    w_value = gaussian(arg_keys[6], (D, D), D ** -0.5, 0.21875, ((0, 4), (1, 4)))
    b_value = gaussian(arg_keys[7], (D,), 0.05, 0.25, (), jnp.float32)
    w_out = gaussian(arg_keys[8], (D, D), 8 ** -0.5, 2.0, ((0, 4), (1, 4)))
    b_out = gaussian(arg_keys[9], (D,), 0.3, 1.5, ((0, 4),), jnp.float32)
    ln2_gain = jnp.clip(1.0 + 0.15 * jax.random.normal(arg_keys[10], (D,), jnp.float32), 0.25, 1.75)
    ln2_bias = gaussian(arg_keys[11], (D,), 0.2, 1.0, ((0, 4),), jnp.float32)
    w_fc1 = gaussian(arg_keys[12], (D, FF), D ** -0.5, 0.21875, ((0, 4), (1, 4)))
    b_fc1 = gaussian(arg_keys[13], (FF,), 0.3, 1.5, (), jnp.float32)
    w_fc2 = gaussian(arg_keys[14], (D, FF), FF ** -0.5, 0.109375, ((0, 4), (1, 4)))
    b_fc2 = gaussian(arg_keys[15], (D,), 0.3, 1.5, ((0, 4),), jnp.float32)
    cotangent = gaussian(arg_keys[16], (CLIPS, SEQ, D), 1.0, 6.0, ((0, 2), (1, 4)))
    return {"frames": frames, "ln1_gain": ln1_gain, "ln1_bias": ln1_bias, "w_query": w_query, "b_query": b_query, "w_key": w_key, "w_value": w_value, "b_value": b_value, "w_out": w_out, "b_out": b_out, "ln2_gain": ln2_gain, "ln2_bias": ln2_bias, "w_fc1": w_fc1, "b_fc1": b_fc1, "w_fc2": w_fc2, "b_fc2": b_fc2, "cotangent": cotangent}


@jax.custom_vjp
def low(v):
    return lax.optimization_barrier(v.astype(jnp.bfloat16)).astype(jnp.float32)

@jax.custom_vjp
def low_back(v):
    return v

def low_keep(v):
    return (low(v), None)

def low_pass(kept, grad):
    return (grad,)

def back_keep(v):
    return (v, None)

def back_low(kept, grad):
    return (low(grad),)
low.defvjp(low_keep, low_pass)
low_back.defvjp(back_keep, back_low)

def product(first_op, second_op):
    return jnp.dot(first_op, second_op, precision=lax.Precision.HIGHEST)

def rounded(tensor):
    return low(low_back(tensor))

def layer_norm(tensor, norm_gain, norm_bias):
    average = lax.optimization_barrier(jnp.mean(tensor, axis=-1, keepdims=True))
    variance = lax.optimization_barrier(jnp.mean(tensor * tensor, axis=-1, keepdims=True)) - average * average
    return (tensor - average) * lax.rsqrt(variance + 1e-05) * norm_gain + norm_bias

def one_head(inputs):
    query_head, key_head, value_head = inputs
    scores = low_back(product(query_head, key_head.T) * 0.125)
    probability = low(jax.nn.softmax(scores, axis=-1))
    return rounded(product(probability, value_head))

def split_heads(tensor):
    return tensor.reshape(SEQ, HEADS, HEAD).transpose(1, 0, 2)

def layer(clip_frames, params):
    ln1_gain, ln1_bias, w_query, b_query, w_key, w_value, b_value, w_out, b_out, ln2_gain, ln2_bias, w_fc1, b_fc1, w_fc2, b_fc2 = params
    normed = low(layer_norm(clip_frames, ln1_gain, ln1_bias))
    query_all = rounded(product(normed, w_query) + b_query)
    key_all = rounded(product(normed, w_key))
    value_all = rounded(product(normed, w_value) + b_value)
    attended = lax.map(jax.checkpoint(one_head), (split_heads(query_all), split_heads(key_all), split_heads(value_all)))
    attended = attended.transpose(1, 0, 2).reshape(SEQ, D)
    residual = clip_frames + low_back(product(attended, w_out) + b_out)
    normed_two = low(layer_norm(residual, ln2_gain, ln2_bias))
    pre_act = low_back(product(normed_two, w_fc1) + b_fc1)
    hidden = low(jax.nn.gelu(pre_act, approximate=False))
    return residual + low_back(product(hidden, w_fc2.T) + b_fc2)

def reference(frames, ln1_gain, ln1_bias, w_query, b_query, w_key, w_value, b_value, w_out, b_out, ln2_gain, ln2_bias, w_fc1, b_fc1, w_fc2, b_fc2, cotangent):
    params = tuple((element.astype(jnp.float32) for element in (ln1_gain, ln1_bias, w_query, b_query, w_key, w_value, b_value, w_out, b_out, ln2_gain, ln2_bias, w_fc1, b_fc1, w_fc2, b_fc2)))
    zeros = tuple((jnp.zeros(element.shape, jnp.float32) for element in params))

    def step(totals, inputs):
        clip_frames, clip_grad = inputs
        result, pullback = jax.vjp(layer, clip_frames.astype(jnp.float32), params)
        grad_clip, grad_params = pullback(clip_grad.astype(jnp.float32))
        totals = tuple((summed + update for summed, update in zip(totals, grad_params)))
        return (totals, (result.astype(jnp.bfloat16), grad_clip.astype(jnp.bfloat16)))
    totals, (outputs, grad_inputs) = lax.scan(step, zeros, (frames, cotangent))
    return (outputs, grad_inputs, totals[0], totals[1], totals[2], totals[3], totals[4], totals[5], totals[6], totals[7], totals[8], totals[9], totals[10], totals[11], totals[12], totals[13], totals[14])
```

```python
import functools
import jax
import jax.numpy as jnp
from jax import lax
from jax.experimental import pallas as pl
from jax.experimental.pallas import tpu as pltpu
from jax.sharding import PartitionSpec as P

HEAD = 64
VMEM_LIMIT = 48 * 1024 * 1024


def mix(first, second, first_dim, second_dim):
    return lax.dot_general(
        first,
        second,
        (((first_dim,), (second_dim,)), ((), ())),
        preferred_element_type=jnp.float32,
    )


def gather_frames(tensor):
    return lax.all_gather(tensor, "col", axis=0, tiled=True)


def reduce_frames(tensor):
    return lax.psum_scatter(
        tensor.astype(jnp.bfloat16), "col", scatter_dimension=0, tiled=True
    ).astype(jnp.float32)


def gather_rows(tensor):
    return lax.all_gather(tensor, "row", axis=0, tiled=True)


def reduce_rows(tensor):
    return lax.psum_scatter(
        tensor.astype(jnp.bfloat16), "row", scatter_dimension=0, tiled=True
    ).astype(jnp.float32)


def all_clips(tensor):
    return lax.psum(tensor.astype(jnp.bfloat16), "dp").astype(jnp.float32)


def place_piece(vector, piece_index, piece_count):
    piece_size = vector.shape[0]
    filled = jnp.zeros((piece_size * piece_count,), jnp.float32)
    return lax.dynamic_update_slice(filled, vector, (piece_index * piece_size,))


def take_piece(vector, piece_index, piece_size):
    return lax.dynamic_slice_in_dim(vector, piece_index * piece_size, piece_size)


def gelu_exact(tensor):
    return jax.nn.gelu(tensor, approximate=False)


def norm_forward(tensor, norm_gain, norm_bias):
    average = jnp.mean(tensor, axis=-1, keepdims=True)
    variance = jnp.mean(tensor * tensor, axis=-1, keepdims=True) - average * average
    inv_std = lax.rsqrt(variance + 1e-05)
    scaled = (tensor - average) * inv_std
    return ((scaled * norm_gain + norm_bias).astype(jnp.bfloat16), scaled, inv_std)


def norm_backward(gradient, scaled, inv_std, norm_gain):
    weighted = gradient * norm_gain
    first_mean = jnp.mean(weighted, axis=-1, keepdims=True)
    second_mean = jnp.mean(weighted * scaled, axis=-1, keepdims=True)
    grad_in = inv_std * (weighted - first_mean - scaled * second_mean)
    return (grad_in, jnp.sum(gradient * scaled, axis=0), jnp.sum(gradient, axis=0))


def query_tile(count):
    for tile in (256, 128, 64, 32, 16):
        if count % tile == 0:
            return tile
    return count


def attend_kernel(query_ref, key_ref, value_ref, mask_ref, out_ref, total_ref):
    heads = query_ref.shape[1] // HEAD
    queries = query_ref[...]
    mask = mask_ref[...]
    outs = []
    totals = []
    for head in range(heads):
        span = slice(head * HEAD, (head + 1) * HEAD)
        scores = mix(queries[:, span], key_ref[:, span], 1, 1) * 0.125 + mask
        highest = jnp.max(scores, axis=-1, keepdims=True)
        powers = jnp.exp(scores - highest)
        total = jnp.sum(powers, axis=-1, keepdims=True)
        probability = (powers * (1.0 / total)).astype(jnp.bfloat16)
        outs.append(mix(probability, value_ref[:, span], 1, 0))
        totals.append(highest + jnp.log(total))
    out_ref[...] = jnp.concatenate(outs, axis=1).astype(jnp.bfloat16)
    total_ref[...] = jnp.concatenate(totals, axis=1)


def attend(queries, keys, values, mask):
    count, width = queries.shape
    heads = width // HEAD
    tile = query_tile(count)
    whole = lambda step: (0, 0)
    part = lambda step: (step, 0)
    return pl.pallas_call(
        attend_kernel,
        grid=(count // tile,),
        in_specs=[
            pl.BlockSpec((tile, width), part),
            pl.BlockSpec(keys.shape, whole),
            pl.BlockSpec(values.shape, whole),
            pl.BlockSpec(mask.shape, whole),
        ],
        out_specs=[pl.BlockSpec((tile, width), part), pl.BlockSpec((tile, heads), part)],
        out_shape=[
            jax.ShapeDtypeStruct((count, width), jnp.bfloat16),
            jax.ShapeDtypeStruct((count, heads), jnp.float32),
        ],
        compiler_params=pltpu.CompilerParams(vmem_limit_bytes=VMEM_LIMIT),
        cost_estimate=pl.CostEstimate(
            flops=4 * count * keys.shape[0] * width,
            bytes_accessed=4 * (count + keys.shape[0]) * width,
            transcendentals=count * keys.shape[0] * heads,
        ),
        name="attend",
    )(queries, keys, values, mask)


def attend_back_kernel(
    query_ref,
    key_ref,
    value_ref,
    mask_ref,
    total_ref,
    grad_ref,
    d_query_ref,
    d_key_ref,
    d_value_ref,
):
    heads = query_ref.shape[1] // HEAD
    queries = query_ref[...]
    grads = grad_ref[...]
    mask = mask_ref[...]
    totals = total_ref[...]

    @pl.when(pl.program_id(0) == 0)
    def _():
        d_key_ref[...] = jnp.zeros_like(d_key_ref)
        d_value_ref[...] = jnp.zeros_like(d_value_ref)

    d_queries = []
    d_keys = []
    d_values = []
    for head in range(heads):
        span = slice(head * HEAD, (head + 1) * HEAD)
        query = queries[:, span]
        grad = grads[:, span]
        key = key_ref[:, span]
        value = value_ref[:, span]
        scores = mix(query, key, 1, 1) * 0.125 + mask
        probability = jnp.exp(scores - totals[:, head : head + 1])
        grad_prob = mix(grad, value, 1, 1)
        row_dot = jnp.sum(probability * grad_prob, axis=-1, keepdims=True)
        grad_scores = (probability * (grad_prob - row_dot)).astype(jnp.bfloat16)
        d_queries.append(mix(grad_scores, key, 1, 0) * 0.125)
        d_keys.append(mix(grad_scores, query, 0, 0) * 0.125)
        d_values.append(mix(probability.astype(jnp.bfloat16), grad, 0, 0))
    d_query_ref[...] = jnp.concatenate(d_queries, axis=1).astype(jnp.bfloat16)
    d_key_ref[...] += jnp.concatenate(d_keys, axis=1)
    d_value_ref[...] += jnp.concatenate(d_values, axis=1)


def attend_back(queries, keys, values, mask, totals, grads):
    count, width = queries.shape
    heads = width // HEAD
    tile = query_tile(count)
    whole = lambda step: (0, 0)
    part = lambda step: (step, 0)
    return pl.pallas_call(
        attend_back_kernel,
        grid=(count // tile,),
        in_specs=[
            pl.BlockSpec((tile, width), part),
            pl.BlockSpec(keys.shape, whole),
            pl.BlockSpec(values.shape, whole),
            pl.BlockSpec(mask.shape, whole),
            pl.BlockSpec((tile, heads), part),
            pl.BlockSpec((tile, width), part),
        ],
        out_specs=[
            pl.BlockSpec((tile, width), part),
            pl.BlockSpec(keys.shape, whole),
            pl.BlockSpec(values.shape, whole),
        ],
        out_shape=[
            jax.ShapeDtypeStruct((count, width), jnp.bfloat16),
            jax.ShapeDtypeStruct(keys.shape, jnp.float32),
            jax.ShapeDtypeStruct(values.shape, jnp.float32),
        ],
        compiler_params=pltpu.CompilerParams(vmem_limit_bytes=VMEM_LIMIT),
        cost_estimate=pl.CostEstimate(
            flops=10 * count * keys.shape[0] * width,
            bytes_accessed=8 * (count + keys.shape[0]) * width,
            transcendentals=count * keys.shape[0] * heads,
        ),
        name="attend_back",
    )(queries, keys, values, mask, totals, grads)


def local(
    frames,
    ln1_gain,
    ln1_bias,
    w_query,
    b_query,
    w_key,
    w_value,
    b_value,
    w_out,
    b_out,
    ln2_gain,
    ln2_bias,
    w_fc1,
    b_fc1,
    w_fc2,
    b_fc2,
    cotangent,
):
    row_count = lax.axis_size("row")
    col_count = lax.axis_size("col")
    row_at = lax.axis_index("row")
    col_at = lax.axis_index("col")
    head_width = w_query.shape[1]
    hidden_part = w_fc1.shape[1]
    clip_count, frame_count, width = frames.shape
    feature_part = width // row_count
    parts = row_count // clip_count
    slot = -(-frame_count // (parts * 64)) * 64
    padding = ((0, 0), (0, slot * parts - frame_count), (0, 0))
    clip_at = row_at // parts
    part_at = row_at % parts

    def own_frames(tensor):
        piece = lax.dynamic_slice(
            jnp.pad(tensor, padding), (clip_at, part_at * slot, 0), (1, slot, width)
        )
        return piece[0]

    def shifted(tensor, shift):
        pairs = [
            (clip * parts + part, clip * parts + (part + shift) % parts)
            for clip in range(clip_count)
            for part in range(parts)
        ]
        return lax.ppermute(tensor, "row", pairs)

    def part_mask(part):
        real = part * slot + jnp.arange(slot) < frame_count
        return jnp.tile(jnp.where(real, 0.0, -1e30).astype(jnp.float32), col_count)

    early = gather_rows(jnp.concatenate([w_query, w_key, w_value, w_out.T], axis=1))
    vectors = gather_rows(
        jnp.stack([ln1_gain, ln1_bias, ln2_gain, ln2_bias, b_out, b_fc2], axis=1)
    ).T
    gain_one, bias_one, gain_two, bias_two, bias_out, bias_last = vectors
    late = gather_rows(jnp.concatenate([w_fc1, w_fc2], axis=1))
    joint_end = 3 * head_width
    w_joint = early[:, :joint_end]
    out_rows = early[:, joint_end:]
    first_ff = late[:, :hidden_part]
    second_ff = late[:, hidden_part:]
    bias_query = take_piece(b_query, col_at, head_width)
    bias_value = take_piece(b_value, col_at, head_width)
    bias_hidden = take_piece(b_fc1, col_at, hidden_part)
    offsets = jnp.concatenate([bias_query, jnp.zeros_like(bias_query), bias_value])

    inputs_wide = own_frames(frames).astype(jnp.float32)
    cotangent_part = own_frames(cotangent)
    normed, scaled_one, inv_std_one = norm_forward(inputs_wide, gain_one, bias_one)
    normed_all = gather_frames(normed)
    cotangent_all = gather_frames(cotangent_part)
    projected = (mix(normed_all, w_joint, 1, 0) + offsets).astype(jnp.bfloat16)
    query_part = projected[:, :head_width]
    pair_part = projected[:, head_width:]
    pair_whole = jnp.concatenate(
        [pair_part] + [shifted(pair_part, shift) for shift in range(1, parts)], axis=0
    )
    mask = jnp.concatenate([part_mask((part_at - shift) % parts) for shift in range(parts)])[None]
    key_whole = pair_whole[:, :head_width]
    value_whole = pair_whole[:, head_width:]
    attended, log_total = attend(query_part, key_whole, value_whole, mask)
    branch = reduce_frames(mix(attended, out_rows, 1, 1))
    residual = inputs_wide + branch + bias_out
    normed_two, scaled_two, inv_std_two = norm_forward(residual, gain_two, bias_two)
    normed_two_all = gather_frames(normed_two)
    pre_act = mix(normed_two_all, first_ff, 1, 0) + bias_hidden
    activated, gelu_pull = jax.vjp(gelu_exact, pre_act)
    hidden = activated.astype(jnp.bfloat16)
    block_part = (residual + reduce_frames(mix(hidden, second_ff, 1, 1)) + bias_last).astype(
        jnp.bfloat16
    )
    hidden_terms = mix(cotangent_all, second_ff, 1, 0)
    d_pre = gelu_pull(hidden_terms)[0].astype(jnp.bfloat16)
    d_normed_two = reduce_frames(mix(d_pre, first_ff, 1, 1))
    grad_second = mix(cotangent_all, hidden, 0, 0)
    grad_first = mix(normed_two_all, d_pre, 0, 0)
    late_grads = all_clips(reduce_rows(jnp.concatenate([grad_first, grad_second], axis=1)))
    d_residual_norm, gain_two_part, bias_two_part = norm_backward(
        d_normed_two, scaled_two, inv_std_two, gain_two
    )
    d_residual = cotangent_part.astype(jnp.float32) + d_residual_norm
    d_branch = d_residual.astype(jnp.bfloat16)
    d_branch_all = gather_frames(d_branch)
    d_attended = mix(d_branch_all, out_rows, 1, 0).astype(jnp.bfloat16)
    d_query, key_grads, value_grads = attend_back(
        query_part, key_whole, value_whole, mask, log_total, d_attended
    )
    grad_out_rows = mix(d_branch_all, attended, 0, 0)
    pair_grads = jnp.concatenate([key_grads, value_grads], axis=1)
    held = query_part.shape[0]
    d_pair = pair_grads[:held]
    for shift in range(1, parts):
        sent = pair_grads[shift * held : (shift + 1) * held].astype(jnp.bfloat16)
        d_pair = d_pair + shifted(sent, parts - shift).astype(jnp.float32)
    d_joint = jnp.concatenate([d_query, d_pair.astype(jnp.bfloat16)], axis=1)
    d_normed = reduce_frames(mix(d_joint, w_joint, 1, 1))
    grad_joint = mix(normed_all, d_joint, 0, 0)
    early_grads = all_clips(reduce_rows(jnp.concatenate([grad_joint, grad_out_rows], axis=1)))
    d_frames_norm, gain_one_part, bias_one_part = norm_backward(
        d_normed, scaled_one, inv_std_one, gain_one
    )
    grad_part = (d_residual + d_frames_norm).astype(jnp.bfloat16)
    joint_sums = jnp.sum(d_joint, axis=0, dtype=jnp.float32)
    hidden_sums = jnp.sum(d_pre, axis=0, dtype=jnp.float32)
    featured = jnp.concatenate(
        [
            gain_one_part,
            bias_one_part,
            gain_two_part,
            bias_two_part,
            jnp.sum(d_branch, axis=0, dtype=jnp.float32),
            jnp.sum(cotangent_part, axis=0, dtype=jnp.float32),
        ]
    )
    headed = jnp.concatenate([joint_sums[:head_width], joint_sums[2 * head_width :], hidden_sums])
    sums = lax.psum(
        jnp.concatenate([featured, place_piece(headed, col_at, col_count)]), ("dp", "row", "col")
    )
    featured_sums = take_piece(
        sums[: 6 * width].reshape(6, row_count, feature_part).transpose(1, 0, 2), row_at, 1
    )[0]
    headed_sums = take_piece(sums[6 * width :], col_at, headed.shape[0])

    def whole_frames(piece):
        whole = lax.all_gather(piece, "row", axis=0, tiled=True)
        return whole.reshape(clip_count, parts * slot, width)[:, :frame_count]

    return (
        whole_frames(block_part),
        whole_frames(grad_part),
        featured_sums[0],
        featured_sums[1],
        early_grads[:, :head_width],
        headed_sums[:head_width],
        early_grads[:, head_width : 2 * head_width],
        early_grads[:, 2 * head_width : joint_end],
        headed_sums[head_width : 2 * head_width],
        early_grads[:, joint_end:].T,
        featured_sums[4],
        featured_sums[2],
        featured_sums[3],
        late_grads[:, :hidden_part],
        headed_sums[2 * head_width :],
        late_grads[:, hidden_part:],
        featured_sums[5],
    )


def solution(mesh):
    placed = (
        P("dp", "col", None),
        P("row"),
        P("row"),
        P("row", "col"),
        P(),
        P("row", "col"),
        P("row", "col"),
        P(),
        P("col", "row"),
        P("row"),
        P("row"),
        P("row"),
        P("row", "col"),
        P(),
        P("row", "col"),
        P("row"),
        P("dp", "col", None),
    )
    return jax.shard_map(
        local,
        mesh=mesh,
        in_specs=placed,
        out_specs=(
            P("dp", "col", None),
            P("dp", "col", None),
            P("row"),
            P("row"),
            P("row", "col"),
            P("col"),
            P("row", "col"),
            P("row", "col"),
            P("col"),
            P("col", "row"),
            P("row"),
            P("row"),
            P("row"),
            P("row", "col"),
            P("col"),
            P("row", "col"),
            P("row"),
        ),
        check_vma=False,
    )
```

```python
import functools
import jax
import jax.numpy as jnp
from jax import lax
from jax.experimental import pallas as pl
from jax.experimental.pallas import tpu as pltpu
from jax.sharding import PartitionSpec as P

HEAD = 64
VMEM_LIMIT = 48 * 1024 * 1024


def mix(first, second, first_dim, second_dim):
    return lax.dot_general(
        first,
        second,
        (((first_dim,), (second_dim,)), ((), ())),
        preferred_element_type=jnp.float32,
    )


def gather_rows(tensor):
    return lax.all_gather(tensor, "row", axis=0, tiled=True)


def reduce_rows(tensor):
    return lax.psum_scatter(
        tensor.astype(jnp.bfloat16), "row", scatter_dimension=0, tiled=True
    ).astype(jnp.float32)


def all_clips(tensor):
    return lax.psum(tensor.astype(jnp.bfloat16), "dp").astype(jnp.float32)


def place_piece(vector, piece_index, piece_count):
    piece_size = vector.shape[0]
    filled = jnp.zeros((piece_size * piece_count,), jnp.float32)
    return lax.dynamic_update_slice(filled, vector, (piece_index * piece_size,))


def take_piece(vector, piece_index, piece_size):
    return lax.dynamic_slice_in_dim(vector, piece_index * piece_size, piece_size)


def put(src, dst, send, recv, axis, index):
    return pltpu.make_async_remote_copy(
        src_ref=src,
        dst_ref=dst,
        send_sem=send,
        recv_sem=recv,
        device_id={axis: index},
        device_id_type=pl.DeviceIdType.MESH,
    )


def ring(me, step, count):
    return lax.rem(me + step, count)


def span(index, size):
    return pl.ds(pl.multiple_of(index * size, size), size)


class Gather:
    def __init__(self, axis, count, source, whole, sends, recvs, row):
        self.axis, self.count, self.me = axis, count, lax.axis_index(axis)
        self.source, self.whole, self.row = source, whole, row
        self.sends, self.recvs = sends, recvs

    def copy(self, step):
        size = self.source.shape[0]
        return put(
            self.source,
            self.whole.at[span(self.me, size)],
            self.sends.at[self.row, step - 1],
            self.recvs.at[self.row, step - 1],
            self.axis,
            ring(self.me, step, self.count),
        )

    def start(self):
        for step in range(1, self.count):
            self.copy(step).start()

    def keep_own(self):
        self.whole[span(self.me, self.source.shape[0]), :] = self.source[...]

    def wait(self):
        for step in range(1, self.count):
            self.copy(step).wait_recv()

    def finish(self):
        for step in range(1, self.count):
            self.copy(step).wait_send()


class Reduce:
    def __init__(self, axis, count, outgoing, incoming, sends, recvs, row, toward=1):
        self.axis, self.count, self.me = axis, count, lax.axis_index(axis)
        self.outgoing, self.incoming, self.row = outgoing, incoming, row
        self.sends, self.recvs, self.toward = sends, recvs, toward

    def copy(self, step):
        ahead = step if self.toward > 0 else self.count - step
        return put(
            self.outgoing.at[step - 1],
            self.incoming.at[step - 1],
            self.sends.at[self.row, step - 1],
            self.recvs.at[self.row, step - 1],
            self.axis,
            ring(self.me, ahead, self.count),
        )

    def send(self, step, value):
        self.outgoing[step - 1] = value.astype(self.outgoing.dtype)
        self.copy(step).start()

    def total(self, own):
        for step in range(1, self.count):
            self.copy(step).wait_recv()
            own = own + self.incoming[step - 1].astype(jnp.float32)
        return own

    def finish(self):
        for step in range(1, self.count):
            self.copy(step).wait_send()


def greet(peers):
    barrier = pltpu.get_barrier_semaphore()
    for axis, index in peers:
        pl.semaphore_signal(
            barrier, inc=1, device_id={axis: index}, device_id_type=pl.DeviceIdType.MESH
        )
    pl.semaphore_wait(barrier, len(peers))


def others(axis, count):
    me = lax.axis_index(axis)
    return [(axis, ring(me, step, count)) for step in range(1, count)]


def partner_row():
    me = lax.axis_index("row")
    return me + 1 - 2 * lax.rem(me, 2)


def norm_stats(tensor):
    average = jnp.mean(tensor, axis=-1, keepdims=True)
    variance = jnp.mean(tensor * tensor, axis=-1, keepdims=True) - average * average
    inv_std = lax.rsqrt(variance + 1e-05)
    return (tensor - average) * inv_std, inv_std


def norm_backward(gradient, scaled, inv_std, norm_gain):
    weighted = gradient * norm_gain
    first_mean = jnp.mean(weighted, axis=-1, keepdims=True)
    second_mean = jnp.mean(weighted * scaled, axis=-1, keepdims=True)
    return inv_std * (weighted - first_mean - scaled * second_mean)


def column_sums(tensor):
    return jnp.sum(tensor, axis=0, keepdims=True)


def front_kernel(
    n_row, n_col,
    x_ref, vec_ref, wq_ref, wkv_ref, wo_ref, bq_ref, bkv_ref, mask_ref,
    vec_out, wq_out, wkv_out, wo_out, normed_out, query_out, pair_out, att_out, total_out,
    resid_out, normed2_out,
    vec_buf, wq_buf, wkv_buf, wo_buf, own_buf, normed_buf, pair_buf, away_buf, sum_out, sum_in,
    own_sum, sends, recvs, pair_sends, pair_recvs,
):
    slot = x_ref.shape[0]
    head_width = wq_ref.shape[1]
    held = slot * n_col
    col_at = lax.axis_index("col")
    partner = partner_row()
    greet(others("row", n_row) + others("col", n_col))
    vec = Reduce("row", n_row, None, vec_buf, sends, recvs, 0)
    vec_copies = [
        put(vec_ref, vec_buf.at[step - 1], sends.at[0, step - 1], recvs.at[0, step - 1], "row",
            ring(vec.me, step, n_row))
        for step in range(1, n_row)
    ]
    for copy in vec_copies:
        copy.start()
    gathers = [
        Gather("row", n_row, wq_ref, wq_buf, sends, recvs, 1),
        Gather("row", n_row, wkv_ref, wkv_buf, sends, recvs, 2),
        Gather("row", n_row, wo_ref, wo_buf, sends, recvs, 3),
    ]
    for gather in gathers:
        gather.start()
    scaled, _ = norm_stats(x_ref[...].astype(jnp.float32))
    vectors = vec_ref[...]
    for step, copy in enumerate(vec_copies):
        copy.wait_recv()
        vectors = vectors + vec_buf[step]
    vec_out[...] = vectors
    own_buf[...] = (scaled * vectors[0:1] + vectors[1:2]).astype(jnp.bfloat16)
    frames = Gather("col", n_col, own_buf, normed_buf, sends, recvs, 4)
    frames.start()
    frames.keep_own()
    for gather in gathers:
        gather.keep_own()
    for gather in gathers:
        gather.wait()

    def pair_copy(at):
        return put(
            pair_buf.at[span(at, slot)],
            away_buf.at[span(at, slot)],
            pair_sends.at[at],
            pair_recvs.at[at],
            "row",
            partner,
        )

    def project(step, carry):
        sender = ring(col_at, n_col - step, n_col)

        @pl.when(step > 0)
        def _():
            frames.copy(step).wait_recv()

        block = normed_buf[span(sender, slot), :]
        normed_out[span(sender, slot), :] = block
        query_out[span(sender, slot), :] = (
            mix(block, wq_buf[...], 1, 0) + bq_ref[...]
        ).astype(jnp.bfloat16)
        pair_buf[span(sender, slot), :] = (
            mix(block, wkv_buf[...], 1, 0) + bkv_ref[...]
        ).astype(jnp.bfloat16)
        pair_copy(sender).start()
        return carry

    lax.fori_loop(0, n_col, project, 0)
    for at in range(n_col):
        pair_copy(at).wait_recv()
    pair_out[0:held, :] = pair_buf[...]
    pair_out[held : 2 * held, :] = away_buf[...]
    sums = Reduce("col", n_col, sum_out, sum_in, sends, recvs, 5)
    mask = mask_ref[...]

    def attend(step, carry):
        owner = ring(col_at, step, n_col)
        queries = query_out[span(owner, slot), :]
        outs = []
        totals = []
        for head in range(head_width // HEAD):
            low = head * HEAD
            key = pair_out[:, low : low + HEAD]
            value = pair_out[:, head_width + low : head_width + low + HEAD]
            scores = mix(queries[:, low : low + HEAD], key, 1, 1) * 0.125 + mask
            highest = jnp.max(scores, axis=-1, keepdims=True)
            powers = jnp.exp(scores - highest)
            total = jnp.sum(powers, axis=-1, keepdims=True)
            probability = (powers * (1.0 / total)).astype(jnp.bfloat16)
            outs.append(mix(probability, value, 1, 0))
            totals.append(highest + jnp.log(total))
        attended = jnp.concatenate(outs, axis=1).astype(jnp.bfloat16)
        att_out[span(owner, slot), :] = attended
        total_out[span(owner, slot), :] = jnp.concatenate(totals, axis=1)
        partial = mix(attended, wo_buf[...], 1, 1)

        @pl.when(step < n_col)
        def _():
            sums.send(step, partial)

        @pl.when(step == n_col)
        def _():
            own_sum[...] = partial

        return carry

    lax.fori_loop(1, n_col + 1, attend, 0)
    wq_out[...] = wq_buf[...]
    wkv_out[...] = wkv_buf[...]
    wo_out[...] = wo_buf[...]
    residual = x_ref[...].astype(jnp.float32) + sums.total(own_sum[...]) + vectors[4:5]
    resid_out[...] = residual
    scaled, _ = norm_stats(residual)
    normed2_out[...] = (scaled * vectors[2:3] + vectors[3:4]).astype(jnp.bfloat16)
    for copy in vec_copies:
        copy.wait_send()
    for gather in gathers:
        gather.finish()
    frames.finish()
    for at in range(n_col):
        pair_copy(at).wait_send()
    sums.finish()


def middle_kernel(
    n_col,
    normed2_ref, resid_ref, cot_ref, cot_all_ref, w1_ref, w2_ref, vec_ref, bh_ref,
    block_out, d_branch_out, d_resid_out, g1_out, g2_out, small_out, hidden_sum_out,
    normed_buf, hidden_buf, d_pre_buf, d_own, d_buf, sum_out, sum_in, own_sum, last_out, last_in,
    own_last, sends, recvs,
):
    slot = resid_ref.shape[0]
    col_at = lax.axis_index("col")
    greet(others("col", n_col))
    frames = Gather("col", n_col, normed2_ref, normed_buf, sends, recvs, 0)
    frames.start()
    frames.keep_own()
    sums = Reduce("col", n_col, sum_out, sum_in, sends, recvs, 1, -1)
    lasts = Reduce("col", n_col, last_out, last_in, sends, recvs, 2, -1)

    def feed(step, carry):
        sender = ring(col_at, n_col - step, n_col)

        @pl.when(step > 0)
        def _():
            frames.copy(step).wait_recv()

        block = normed_buf[span(sender, slot), :]
        pre = mix(block, w1_ref[...], 1, 0) + bh_ref[...]
        normal = 0.5 * (1.0 + lax.erf(pre * 0.7071067811865476))
        hidden = (pre * normal).astype(jnp.bfloat16)
        hidden_buf[span(sender, slot), :] = hidden
        slope = normal + pre * (0.3989422804014327 * jnp.exp(-0.5 * pre * pre))
        terms = mix(cot_all_ref[span(sender, slot), :], w2_ref[...], 1, 0)
        d_pre = (terms * slope).astype(jnp.bfloat16)
        d_pre_buf[span(sender, slot), :] = d_pre
        partial = mix(d_pre, w1_ref[...], 1, 1)

        @pl.when(step > 0)
        def _():
            sums.send(step, partial)

        @pl.when(step == 0)
        def _():
            own_sum[...] = partial

        return carry

    lax.fori_loop(0, n_col, feed, 0)
    scaled, inv_std = norm_stats(resid_ref[...])
    d_normed = sums.total(own_sum[...])
    d_resid = cot_ref[...].astype(jnp.float32) + norm_backward(
        d_normed, scaled, inv_std, vec_ref[2:3, :]
    )
    d_resid_out[...] = d_resid
    d_own[...] = d_resid.astype(jnp.bfloat16)
    backs = Gather("col", n_col, d_own, d_buf, sends, recvs, 3)
    backs.start()
    backs.keep_own()
    def finish_block(step, carry):
        sender = ring(col_at, n_col - step, n_col)
        partial = mix(hidden_buf[span(sender, slot), :], w2_ref[...], 1, 1)

        @pl.when(step > 0)
        def _():
            lasts.send(step, partial)

        @pl.when(step == 0)
        def _():
            own_last[...] = partial

        return carry

    lax.fori_loop(0, n_col, finish_block, 0)
    g1_out[...] = mix(normed_buf[...], d_pre_buf[...], 0, 0).astype(jnp.bfloat16)
    g2_out[...] = mix(cot_all_ref[...], hidden_buf[...], 0, 0).astype(jnp.bfloat16)
    hidden_sum_out[...] = column_sums(d_pre_buf[...].astype(jnp.float32))
    small_out[...] = jnp.concatenate(
        [
            column_sums(d_normed * scaled),
            column_sums(d_normed),
            column_sums(d_own[...].astype(jnp.float32)),
            column_sums(cot_ref[...].astype(jnp.float32)),
        ],
        axis=0,
    )
    backs.wait()
    d_branch_out[...] = d_buf[...]
    block_out[...] = (
        resid_ref[...] + lasts.total(own_last[...]) + vec_ref[5:6, :]
    ).astype(jnp.bfloat16)
    frames.finish()
    sums.finish()
    lasts.finish()
    backs.finish()


def back_kernel(
    n_col,
    x_ref, d_resid_ref, vec_ref, wq_ref, wkv_ref, wo_ref, normed_ref, query_ref, pair_ref,
    att_ref, total_ref, mask_ref, d_branch_ref,
    frames_out, small_out, bq_out, bkv_out, gq_out, gkv_out, go_out,
    d_query_buf, d_key_buf, d_value_buf, pair_buf, away_buf, d_pair_buf, sum_out, sum_in, own_sum,
    sends, recvs, pair_sends, pair_recvs,
):
    slot = x_ref.shape[0]
    head_width = wq_ref.shape[1]
    held = slot * n_col
    col_at = lax.axis_index("col")
    partner = partner_row()
    greet([("row", partner)] + others("col", n_col))
    d_key_buf[...] = jnp.zeros_like(d_key_buf)
    d_value_buf[...] = jnp.zeros_like(d_value_buf)
    mask = mask_ref[...]

    def attend_back(at, carry):
        grads = mix(d_branch_ref[span(at, slot), :], wo_ref[...], 1, 0).astype(jnp.bfloat16)
        queries = query_ref[span(at, slot), :]
        totals = total_ref[span(at, slot), :]
        d_queries = []
        d_keys = []
        d_values = []
        for head in range(head_width // HEAD):
            low = head * HEAD
            query = queries[:, low : low + HEAD]
            grad = grads[:, low : low + HEAD]
            key = pair_ref[:, low : low + HEAD]
            value = pair_ref[:, head_width + low : head_width + low + HEAD]
            scores = mix(query, key, 1, 1) * 0.125 + mask
            probability = jnp.exp(scores - totals[:, head : head + 1])
            grad_prob = mix(grad, value, 1, 1)
            row_dot = jnp.sum(probability * grad_prob, axis=-1, keepdims=True)
            grad_scores = (probability * (grad_prob - row_dot)).astype(jnp.bfloat16)
            d_queries.append(mix(grad_scores, key, 1, 0) * 0.125)
            d_keys.append(mix(grad_scores, query, 0, 0) * 0.125)
            d_values.append(mix(probability.astype(jnp.bfloat16), grad, 0, 0))
        d_query_buf[span(at, slot), :] = jnp.concatenate(d_queries, axis=1).astype(jnp.bfloat16)
        d_key_buf[...] += jnp.concatenate(d_keys, axis=1)
        d_value_buf[...] += jnp.concatenate(d_values, axis=1)
        return carry

    lax.fori_loop(0, n_col, attend_back, 0)
    pair_buf[0] = d_key_buf[held : 2 * held, :].astype(jnp.bfloat16)
    pair_buf[1] = d_value_buf[held : 2 * held, :].astype(jnp.bfloat16)
    crossing = put(pair_buf, away_buf, pair_sends.at[0], pair_recvs.at[0], "row", partner)
    crossing.start()
    gq_out[...] = mix(normed_ref[...], d_query_buf[...], 0, 0).astype(jnp.bfloat16)
    go_out[...] = mix(d_branch_ref[...], att_ref[...], 0, 0).astype(jnp.bfloat16)
    crossing.wait_recv()
    d_key = d_key_buf[0:held, :] + away_buf[0].astype(jnp.float32)
    d_value = d_value_buf[0:held, :] + away_buf[1].astype(jnp.float32)
    d_pair_buf[...] = jnp.concatenate([d_key, d_value], axis=1).astype(jnp.bfloat16)
    sums = Reduce("col", n_col, sum_out, sum_in, sends, recvs, 0)

    def spread(step, carry):
        owner = ring(col_at, step, n_col)
        partial = mix(d_query_buf[span(owner, slot), :], wq_ref[...], 1, 1) + mix(
            d_pair_buf[span(owner, slot), :], wkv_ref[...], 1, 1
        )

        @pl.when(step < n_col)
        def _():
            sums.send(step, partial)

        @pl.when(step == n_col)
        def _():
            own_sum[...] = partial

        return carry

    lax.fori_loop(1, n_col + 1, spread, 0)
    gkv_out[...] = mix(normed_ref[...], d_pair_buf[...], 0, 0).astype(jnp.bfloat16)
    bq_out[...] = column_sums(d_query_buf[...].astype(jnp.float32))
    bkv_out[...] = column_sums(d_pair_buf[...].astype(jnp.float32))
    scaled, inv_std = norm_stats(x_ref[...].astype(jnp.float32))
    d_normed = sums.total(own_sum[...])
    frames_out[...] = (
        d_resid_ref[...] + norm_backward(d_normed, scaled, inv_std, vec_ref[0:1, :])
    ).astype(jnp.bfloat16)
    small_out[...] = jnp.concatenate(
        [column_sums(d_normed * scaled), column_sums(d_normed)], axis=0
    )
    crossing.wait_send()
    sums.finish()


def call(kernel, name, number, flops, outs, scratch, *operands):
    return pl.pallas_call(
        kernel,
        in_specs=[pl.BlockSpec(memory_space=pltpu.VMEM)] * len(operands),
        out_specs=[pl.BlockSpec(memory_space=pltpu.VMEM)] * len(outs),
        out_shape=[jax.ShapeDtypeStruct(shape, kind) for shape, kind in outs],
        scratch_shapes=scratch,
        compiler_params=pltpu.CompilerParams(
            vmem_limit_bytes=VMEM_LIMIT, collective_id=number, has_side_effects=True
        ),
        cost_estimate=pl.CostEstimate(flops=flops, bytes_accessed=60000000, transcendentals=0),
        name=name,
    )(*operands)


def local(
    frames,
    ln1_gain,
    ln1_bias,
    w_query,
    b_query,
    w_key,
    w_value,
    b_value,
    w_out,
    b_out,
    ln2_gain,
    ln2_bias,
    w_fc1,
    b_fc1,
    w_fc2,
    b_fc2,
    cotangent,
):
    row_count = lax.axis_size("row")
    col_count = lax.axis_size("col")
    row_at = lax.axis_index("row")
    col_at = lax.axis_index("col")
    head_width = w_query.shape[1]
    hidden_part = w_fc1.shape[1]
    clip_count, frame_count, width = frames.shape
    feature_part = width // row_count
    parts = row_count // clip_count
    slot = -(-frame_count // (parts * 64)) * 64
    padding = ((0, 0), (0, slot * parts - frame_count), (0, 0))
    clip_at = row_at // parts
    part_at = row_at % parts

    def own_frames(tensor):
        piece = lax.dynamic_slice(
            jnp.pad(tensor, padding), (clip_at, part_at * slot, 0), (1, slot, width)
        )
        return piece[0]

    def part_mask(part):
        real = part * slot + jnp.arange(slot) < frame_count
        return jnp.tile(jnp.where(real, 0.0, -1e30).astype(jnp.float32), col_count)

    bf16, f32 = jnp.bfloat16, jnp.float32
    held = slot * col_count
    away = max(row_count, col_count) - 1
    dma = pltpu.SemaphoreType.DMA
    late = gather_rows(jnp.concatenate([w_fc1, w_fc2], axis=1))
    bias_query = take_piece(b_query, col_at, head_width)
    bias_value = take_piece(b_value, col_at, head_width)
    bias_hidden = take_piece(b_fc1, col_at, hidden_part)
    bias_pair = jnp.concatenate([jnp.zeros_like(bias_value), bias_value])
    stacked = jnp.stack(
        [ln1_gain, ln1_bias, ln2_gain, ln2_bias, b_out, b_fc2, jnp.zeros_like(b_out), jnp.zeros_like(b_out)]
    )
    vec_part = lax.dynamic_update_slice(
        jnp.zeros((8, width), f32), stacked, (0, row_at * feature_part)
    )
    inputs_own = own_frames(frames)
    cotangent_part = own_frames(cotangent)
    cotangent_all = lax.all_gather(cotangent_part, "col", axis=0, tiled=True)
    mask = jnp.concatenate([part_mask((part_at - shift) % parts) for shift in range(parts)])[None]
    block = pltpu.VMEM((slot, width), bf16)
    total = pltpu.VMEM((slot, width), f32)
    blocks = pltpu.VMEM((col_count - 1, slot, width), bf16)
    (
        vectors, wq, wkv, wo, normed_all, query_part, pair_whole, attended, log_total, residual,
        normed_two,
    ) = call(
        functools.partial(front_kernel, row_count, col_count), "front", 1, 4 * 10**10,
        [
            ((8, width), f32), ((width, head_width), bf16), ((width, 2 * head_width), bf16),
            ((width, head_width), bf16), ((held, width), bf16), ((held, head_width), bf16),
            ((parts * held, 2 * head_width), bf16), ((held, head_width), bf16),
            ((held, head_width // HEAD), f32), ((slot, width), f32), ((slot, width), bf16),
        ],
        [
            pltpu.VMEM((row_count - 1, 8, width), f32),
            pltpu.VMEM((width, head_width), bf16),
            pltpu.VMEM((width, 2 * head_width), bf16),
            pltpu.VMEM((width, head_width), bf16),
            block,
            pltpu.VMEM((held, width), bf16),
            pltpu.VMEM((held, 2 * head_width), bf16),
            pltpu.VMEM((held, 2 * head_width), bf16),
            blocks, blocks, total,
            dma((6, away)), dma((6, away)), dma((col_count,)), dma((col_count,)),
        ],
        inputs_own, vec_part, w_query, jnp.concatenate([w_key, w_value], axis=1), w_out.T,
        bias_query[None], bias_pair[None], mask,
    )
    block_part, d_branch_all, d_residual, grad_first, grad_second, small_two, hidden_sums = call(
        functools.partial(middle_kernel, col_count), "middle", 2, 4 * 10**10,
        [
            ((slot, width), bf16), ((held, width), bf16), ((slot, width), f32),
            ((width, hidden_part), bf16), ((width, hidden_part), bf16), ((4, width), f32),
            ((1, hidden_part), f32),
        ],
        [
            pltpu.VMEM((held, width), bf16),
            pltpu.VMEM((held, hidden_part), bf16),
            pltpu.VMEM((held, hidden_part), bf16),
            block,
            pltpu.VMEM((held, width), bf16),
            blocks, blocks, total, blocks, blocks, total,
            dma((4, away)), dma((4, away)),
        ],
        normed_two, residual, cotangent_part, cotangent_all, late[:, :hidden_part],
        late[:, hidden_part:], vectors, bias_hidden[None],
    )
    grad_part, small_one, query_sums, pair_sums, grad_q, grad_kv, grad_o = call(
        functools.partial(back_kernel, col_count), "back", 3, 4 * 10**10,
        [
            ((slot, width), bf16), ((2, width), f32), ((1, head_width), f32),
            ((1, 2 * head_width), f32), ((width, head_width), bf16),
            ((width, 2 * head_width), bf16), ((width, head_width), bf16),
        ],
        [
            pltpu.VMEM((held, head_width), bf16),
            pltpu.VMEM((parts * held, head_width), f32),
            pltpu.VMEM((parts * held, head_width), f32),
            pltpu.VMEM((2, held, head_width), bf16),
            pltpu.VMEM((2, held, head_width), bf16),
            pltpu.VMEM((held, 2 * head_width), bf16),
            blocks, blocks, total,
            dma((1, away)), dma((1, away)), dma((1,)), dma((1,)),
        ],
        inputs_own, d_residual, vectors, wq, wkv, wo, normed_all, query_part, pair_whole, attended,
        log_total, mask, d_branch_all,
    )
    joint_end = 3 * head_width
    late_grads = all_clips(reduce_rows(jnp.concatenate([grad_first, grad_second], axis=1)))
    early_grads = all_clips(reduce_rows(jnp.concatenate([grad_q, grad_kv, grad_o], axis=1)))
    featured = jnp.concatenate([small_one, small_two], axis=0).reshape(-1)
    headed = jnp.concatenate([query_sums[0], pair_sums[0, head_width:], hidden_sums[0]])
    sums = lax.psum(
        jnp.concatenate([featured, place_piece(headed, col_at, col_count)]), ("dp", "row", "col")
    )
    featured_sums = take_piece(
        sums[: 6 * width].reshape(6, row_count, feature_part).transpose(1, 0, 2), row_at, 1
    )[0]
    headed_sums = take_piece(sums[6 * width :], col_at, headed.shape[0])

    def whole_frames(piece):
        whole = lax.all_gather(piece, "row", axis=0, tiled=True)
        return whole.reshape(clip_count, parts * slot, width)[:, :frame_count]

    return (
        whole_frames(block_part),
        whole_frames(grad_part),
        featured_sums[0],
        featured_sums[1],
        early_grads[:, :head_width],
        headed_sums[:head_width],
        early_grads[:, head_width : 2 * head_width],
        early_grads[:, 2 * head_width : joint_end],
        headed_sums[head_width : 2 * head_width],
        early_grads[:, joint_end:].T,
        featured_sums[4],
        featured_sums[2],
        featured_sums[3],
        late_grads[:, :hidden_part],
        headed_sums[2 * head_width :],
        late_grads[:, hidden_part:],
        featured_sums[5],
    )


def solution(mesh):
    placed = (
        P("dp", "col", None),
        P("row"),
        P("row"),
        P("row", "col"),
        P(),
        P("row", "col"),
        P("row", "col"),
        P(),
        P("col", "row"),
        P("row"),
        P("row"),
        P("row"),
        P("row", "col"),
        P(),
        P("row", "col"),
        P("row"),
        P("dp", "col", None),
    )
    return jax.shard_map(
        local,
        mesh=mesh,
        in_specs=placed,
        out_specs=(
            P("dp", "col", None),
            P("dp", "col", None),
            P("row"),
            P("row"),
            P("row", "col"),
            P("col"),
            P("row", "col"),
            P("row", "col"),
            P("col"),
            P("col", "row"),
            P("row"),
            P("row"),
            P("row"),
            P("row", "col"),
            P("col"),
            P("row", "col"),
            P("row"),
        ),
        check_vma=False,
    )
```

```python
import functools
import jax
import jax.numpy as jnp
from jax import lax
from jax.experimental import pallas as pl
from jax.experimental.pallas import tpu as pltpu
from jax.sharding import PartitionSpec as P

HEAD = 64
VMEM_LIMIT = 56 * 1024 * 1024


def mix(first, second, first_dim, second_dim):
    return lax.dot_general(
        first,
        second,
        (((first_dim,), (second_dim,)), ((), ())),
        preferred_element_type=jnp.float32,
    )


def gather_rows(tensor):
    return lax.all_gather(tensor, "row", axis=0, tiled=True)


def take_piece(vector, piece_index, piece_size):
    return lax.dynamic_slice_in_dim(vector, piece_index * piece_size, piece_size)


def put(src, dst, send, recv, axis, index):
    return pltpu.make_async_remote_copy(
        src_ref=src,
        dst_ref=dst,
        send_sem=send,
        recv_sem=recv,
        device_id={axis: index},
        device_id_type=pl.DeviceIdType.MESH,
    )


def ring(me, step, count):
    return lax.rem(me + step, count)


def span(index, size):
    return pl.ds(pl.multiple_of(index * size, size), size)


class Gather:
    def __init__(self, axis, count, source, whole, sends, recvs, row):
        self.axis, self.count, self.me = axis, count, lax.axis_index(axis)
        self.source, self.whole, self.row = source, whole, row
        self.sends, self.recvs = sends, recvs

    def copy(self, step):
        size = self.source.shape[0]
        return put(
            self.source,
            self.whole.at[span(self.me, size)],
            self.sends.at[self.row, step - 1],
            self.recvs.at[self.row, step - 1],
            self.axis,
            ring(self.me, step, self.count),
        )

    def start(self):
        for step in range(1, self.count):
            self.copy(step).start()

    def keep_own(self):
        self.whole[span(self.me, self.source.shape[0]), :] = self.source[...]

    def wait(self):
        for step in range(1, self.count):
            self.copy(step).wait_recv()

    def finish(self):
        for step in range(1, self.count):
            self.copy(step).wait_send()


class Scatter:
    def __init__(self, axis, count, source, incoming, sends, recvs, row):
        self.axis, self.count, self.me = axis, count, lax.axis_index(axis)
        self.source, self.incoming, self.row = source, incoming, row
        self.sends, self.recvs = sends, recvs

    def copy(self, step):
        peer = ring(self.me, step, self.count)
        return put(
            self.source.at[span(peer, self.incoming.shape[1])],
            self.incoming.at[step - 1],
            self.sends.at[self.row, step - 1],
            self.recvs.at[self.row, step - 1],
            self.axis,
            peer,
        )

    def start(self):
        for step in range(1, self.count):
            self.copy(step).start()

    def total(self):
        own = self.source[span(self.me, self.incoming.shape[1]), :].astype(jnp.float32)
        for step in range(1, self.count):
            self.copy(step).wait_recv()
            own = own + self.incoming[step - 1].astype(jnp.float32)
        return own

    def finish(self):
        for step in range(1, self.count):
            self.copy(step).wait_send()


class Share(Gather):
    def begin(self, value):
        self.source[...] = value.astype(self.source.dtype)
        self.start()
        self.keep_own()

    def total(self):
        size = self.source.shape[0]
        self.wait()
        result = self.whole[0:size, :].astype(jnp.float32)
        for at in range(1, self.count):
            result = result + self.whole[at * size : (at + 1) * size, :].astype(jnp.float32)
        return result


class Reduce:
    def __init__(self, axis, count, outgoing, incoming, sends, recvs, row, toward=1):
        self.axis, self.count, self.me = axis, count, lax.axis_index(axis)
        self.outgoing, self.incoming, self.row = outgoing, incoming, row
        self.sends, self.recvs, self.toward = sends, recvs, toward

    def copy(self, step):
        ahead = step if self.toward > 0 else self.count - step
        return put(
            self.outgoing.at[step - 1],
            self.incoming.at[step - 1],
            self.sends.at[self.row, step - 1],
            self.recvs.at[self.row, step - 1],
            self.axis,
            ring(self.me, ahead, self.count),
        )

    def send(self, step, value):
        self.outgoing[step - 1] = value.astype(self.outgoing.dtype)
        self.copy(step).start()

    def total(self, own):
        for step in range(1, self.count):
            self.copy(step).wait_recv()
            own = own + self.incoming[step - 1].astype(jnp.float32)
        return own

    def finish(self):
        for step in range(1, self.count):
            self.copy(step).wait_send()


def greet(peers):
    barrier = pltpu.get_barrier_semaphore()
    for axis, index in peers:
        pl.semaphore_signal(
            barrier, inc=1, device_id={axis: index}, device_id_type=pl.DeviceIdType.MESH
        )
    pl.semaphore_wait(barrier, len(peers))


def others(axis, count):
    me = lax.axis_index(axis)
    return [(axis, ring(me, step, count)) for step in range(1, count)]


def partner_row():
    me = lax.axis_index("row")
    return me + 1 - 2 * lax.rem(me, 2)


def norm_stats(tensor):
    average = jnp.mean(tensor, axis=-1, keepdims=True)
    variance = jnp.mean(tensor * tensor, axis=-1, keepdims=True) - average * average
    inv_std = lax.rsqrt(variance + 1e-05)
    return (tensor - average) * inv_std, inv_std


def norm_backward(gradient, scaled, inv_std, norm_gain):
    weighted = gradient * norm_gain
    first_mean = jnp.mean(weighted, axis=-1, keepdims=True)
    second_mean = jnp.mean(weighted * scaled, axis=-1, keepdims=True)
    return inv_std * (weighted - first_mean - scaled * second_mean)


def column_sums(tensor):
    return jnp.sum(tensor, axis=0, keepdims=True)


def front_kernel(
    n_row, n_col,
    x_ref, cot_ref, vec_ref, wq_ref, wkv_ref, wo_ref, bq_ref, bkv_ref, mask_ref,
    vec_out, wq_out, wkv_out, wo_out, normed_out, query_out, pair_out, att_out, total_out,
    resid_out, normed2_out, cot_out,
    cot_buf, vec_buf, wq_buf, wkv_buf, wo_buf, own_buf, normed_buf, pair_buf, away_buf, sum_out, sum_in,
    own_sum, sends, recvs, pair_sends, pair_recvs,
):
    slot = x_ref.shape[0]
    head_width = wq_ref.shape[1]
    held = slot * n_col
    col_at = lax.axis_index("col")
    partner = partner_row()
    greet(others("row", n_row) + others("col", n_col))
    vec = Reduce("row", n_row, None, vec_buf, sends, recvs, 0)
    vec_copies = [
        put(vec_ref, vec_buf.at[step - 1], sends.at[0, step - 1], recvs.at[0, step - 1], "row",
            ring(vec.me, step, n_row))
        for step in range(1, n_row)
    ]
    for copy in vec_copies:
        copy.start()
    gathers = [
        Gather("row", n_row, wq_ref, wq_buf, sends, recvs, 1),
        Gather("row", n_row, wkv_ref, wkv_buf, sends, recvs, 2),
        Gather("row", n_row, wo_ref, wo_buf, sends, recvs, 3),
    ]
    for gather in gathers:
        gather.start()
    scaled, _ = norm_stats(x_ref[...].astype(jnp.float32))
    vectors = vec_ref[...]
    for step, copy in enumerate(vec_copies):
        copy.wait_recv()
        vectors = vectors + vec_buf[step]
    vec_out[...] = vectors
    own_buf[...] = (scaled * vectors[0:1] + vectors[1:2]).astype(jnp.bfloat16)
    frames = Gather("col", n_col, own_buf, normed_buf, sends, recvs, 4)
    frames.start()
    frames.keep_own()
    for gather in gathers:
        gather.keep_own()
    for gather in gathers:
        gather.wait()

    def pair_copy(at):
        return put(
            pair_buf.at[span(at, slot)],
            away_buf.at[span(at, slot)],
            pair_sends.at[at],
            pair_recvs.at[at],
            "row",
            partner,
        )

    def project(step, carry):
        sender = ring(col_at, n_col - step, n_col)

        @pl.when(step > 0)
        def _():
            frames.copy(step).wait_recv()

        block = normed_buf[span(sender, slot), :]
        normed_out[span(sender, slot), :] = block
        query_out[span(sender, slot), :] = (
            mix(block, wq_buf[...], 1, 0) + bq_ref[...]
        ).astype(jnp.bfloat16)
        pair_buf[span(sender, slot), :] = (
            mix(block, wkv_buf[...], 1, 0) + bkv_ref[...]
        ).astype(jnp.bfloat16)
        pair_copy(sender).start()
        return carry

    lax.fori_loop(0, n_col, project, 0)
    cots = Gather("col", n_col, cot_ref, cot_buf, sends, recvs, 6)
    cots.start()
    cots.keep_own()
    for at in range(n_col):
        pair_copy(at).wait_recv()
    pair_out[0:held, :] = pair_buf[...]
    pair_out[held : 2 * held, :] = away_buf[...]
    sums = Reduce("col", n_col, sum_out, sum_in, sends, recvs, 5)
    mask = mask_ref[...]

    def attend(step, carry):
        owner = ring(col_at, step, n_col)
        queries = query_out[span(owner, slot), :]
        outs = []
        totals = []
        for head in range(head_width // HEAD):
            low = head * HEAD
            key = pair_out[:, low : low + HEAD]
            value = pair_out[:, head_width + low : head_width + low + HEAD]
            scores = mix(queries[:, low : low + HEAD], key, 1, 1) * 0.125 + mask
            highest = jnp.max(scores, axis=-1, keepdims=True)
            powers = jnp.exp(scores - highest)
            total = jnp.sum(powers, axis=-1, keepdims=True)
            probability = (powers * (1.0 / total)).astype(jnp.bfloat16)
            outs.append(mix(probability, value, 1, 0))
            totals.append(highest + jnp.log(total))
        attended = jnp.concatenate(outs, axis=1).astype(jnp.bfloat16)
        att_out[span(owner, slot), :] = attended
        total_out[span(owner, slot), :] = jnp.concatenate(totals, axis=1)
        partial = mix(attended, wo_buf[...], 1, 1)

        @pl.when(step < n_col)
        def _():
            sums.send(step, partial)

        @pl.when(step == n_col)
        def _():
            own_sum[...] = partial

        return carry

    lax.fori_loop(1, n_col + 1, attend, 0)
    wq_out[...] = wq_buf[...]
    wkv_out[...] = wkv_buf[...]
    wo_out[...] = wo_buf[...]
    residual = x_ref[...].astype(jnp.float32) + sums.total(own_sum[...]) + vectors[4:5]
    resid_out[...] = residual
    scaled, _ = norm_stats(residual)
    normed2_out[...] = (scaled * vectors[2:3] + vectors[3:4]).astype(jnp.bfloat16)
    cots.wait()
    cot_out[...] = cot_buf[...]
    cots.finish()
    for copy in vec_copies:
        copy.wait_send()
    for gather in gathers:
        gather.finish()
    frames.finish()
    for at in range(n_col):
        pair_copy(at).wait_send()
    sums.finish()


def middle_kernel(
    n_col,
    normed2_ref, resid_ref, cot_ref, cot_all_ref, w1_ref, w2_ref, vec_ref, bh_ref,
    hidden_out, d_branch_out, d_resid_out, g1_out, g2_out, small_out, hidden_sum_out,
    normed_buf, d_pre_buf, d_own, d_buf, sum_out, sum_in, own_sum, sends, recvs,
):
    slot = resid_ref.shape[0]
    col_at = lax.axis_index("col")
    greet(others("col", n_col))
    frames = Gather("col", n_col, normed2_ref, normed_buf, sends, recvs, 0)
    frames.start()
    frames.keep_own()
    sums = Reduce("col", n_col, sum_out, sum_in, sends, recvs, 1, -1)

    def feed(step, carry):
        sender = ring(col_at, n_col - step, n_col)

        @pl.when(step > 0)
        def _():
            frames.copy(step).wait_recv()

        block = normed_buf[span(sender, slot), :]
        pre = mix(block, w1_ref[...], 1, 0) + bh_ref[...]
        normal = 0.5 * (1.0 + lax.erf(pre * 0.7071067811865476))
        hidden = (pre * normal).astype(jnp.bfloat16)
        hidden_out[span(sender, slot), :] = hidden
        slope = normal + pre * (0.3989422804014327 * jnp.exp(-0.5 * pre * pre))
        terms = mix(cot_all_ref[span(sender, slot), :], w2_ref[...], 1, 0)
        d_pre = (terms * slope).astype(jnp.bfloat16)
        d_pre_buf[span(sender, slot), :] = d_pre
        partial = mix(d_pre, w1_ref[...], 1, 1)

        @pl.when(step > 0)
        def _():
            sums.send(step, partial)

        @pl.when(step == 0)
        def _():
            own_sum[...] = partial

        return carry

    lax.fori_loop(0, n_col, feed, 0)
    scaled, inv_std = norm_stats(resid_ref[...])
    d_normed = sums.total(own_sum[...])
    d_resid = cot_ref[...].astype(jnp.float32) + norm_backward(
        d_normed, scaled, inv_std, vec_ref[2:3, :]
    )
    d_resid_out[...] = d_resid
    d_own[...] = d_resid.astype(jnp.bfloat16)
    backs = Gather("col", n_col, d_own, d_buf, sends, recvs, 3)
    backs.start()
    backs.keep_own()
    g1_out[...] = mix(normed_buf[...], d_pre_buf[...], 0, 0).astype(jnp.bfloat16)
    g2_out[...] = mix(cot_all_ref[...], hidden_out[...], 0, 0).astype(jnp.bfloat16)
    hidden_sum_out[...] = column_sums(d_pre_buf[...].astype(jnp.float32))
    small_out[...] = jnp.concatenate(
        [
            column_sums(d_normed * scaled),
            column_sums(d_normed),
            column_sums(d_own[...].astype(jnp.float32)),
            column_sums(cot_ref[...].astype(jnp.float32)),
        ],
        axis=0,
    )
    backs.wait()
    d_branch_out[...] = d_buf[...]
    frames.finish()
    sums.finish()
    backs.finish()


def back_kernel(
    n_dp, n_row, n_col,
    x_ref, d_resid_ref, vec_ref, wq_ref, wkv_ref, wo_ref, normed_ref, query_ref, pair_ref,
    att_ref, total_ref, mask_ref, d_branch_ref, hidden_ref, w2_ref, resid_ref, g1_ref, g2_ref,
    small_two_ref, hidden_sum_ref,
    block_out, frames_out, feature_out, head_out, g1_out, g2_out, gq_out, gkv_out, go_out,
    d_query_buf, d_key_buf, d_value_buf, pair_buf, away_buf, d_pair_buf, sum_out, sum_in, own_sum,
    last_out, last_in, own_last, own_block, block_buf, own_frames, frames_buf,
    gq_buf, gkv_buf, go_buf, g1_in, g2_in, gq_in, gkv_in, go_in,
    g1_own, g2_own, gq_own, gkv_own, go_own, g1_dp, g2_dp, gq_dp, gkv_dp, go_dp,
    feature_own, feature_buf, small_own, small_buf, last_own, last_buf,
    sends, recvs, pair_sends, pair_recvs,
):
    slot = x_ref.shape[0]
    head_width = wq_ref.shape[1]
    held = slot * n_col
    width = x_ref.shape[1]
    col_at = lax.axis_index("col")
    partner = partner_row()
    greet(others("row", n_row) + others("col", n_col) + others("dp", n_dp))
    late = [
        Scatter("row", n_row, g1_ref, g1_in, sends, recvs, 2),
        Scatter("row", n_row, g2_ref, g2_in, sends, recvs, 3),
    ]
    for scatter in late:
        scatter.start()
    lasts = Reduce("col", n_col, last_out, last_in, sends, recvs, 1, -1)

    def finish_block(step, carry):
        sender = ring(col_at, n_col - step, n_col)
        partial = mix(hidden_ref[span(sender, slot), :], w2_ref[...], 1, 1)

        @pl.when(step > 0)
        def _():
            lasts.send(step, partial)

        @pl.when(step == 0)
        def _():
            own_last[...] = partial

        return carry

    lax.fori_loop(0, n_col, finish_block, 0)
    d_key_buf[...] = jnp.zeros_like(d_key_buf)
    d_value_buf[...] = jnp.zeros_like(d_value_buf)
    mask = mask_ref[...]

    def attend_back(at, carry):
        grads = mix(d_branch_ref[span(at, slot), :], wo_ref[...], 1, 0).astype(jnp.bfloat16)
        queries = query_ref[span(at, slot), :]
        totals = total_ref[span(at, slot), :]
        d_queries = []
        d_keys = []
        d_values = []
        for head in range(head_width // HEAD):
            low = head * HEAD
            query = queries[:, low : low + HEAD]
            grad = grads[:, low : low + HEAD]
            key = pair_ref[:, low : low + HEAD]
            value = pair_ref[:, head_width + low : head_width + low + HEAD]
            scores = mix(query, key, 1, 1) * 0.125 + mask
            probability = jnp.exp(scores - totals[:, head : head + 1])
            grad_prob = mix(grad, value, 1, 1)
            row_dot = jnp.sum(probability * grad_prob, axis=-1, keepdims=True)
            grad_scores = (probability * (grad_prob - row_dot)).astype(jnp.bfloat16)
            d_queries.append(mix(grad_scores, key, 1, 0) * 0.125)
            d_keys.append(mix(grad_scores, query, 0, 0) * 0.125)
            d_values.append(mix(probability.astype(jnp.bfloat16), grad, 0, 0))
        d_query_buf[span(at, slot), :] = jnp.concatenate(d_queries, axis=1).astype(jnp.bfloat16)
        d_key_buf[...] += jnp.concatenate(d_keys, axis=1)
        d_value_buf[...] += jnp.concatenate(d_values, axis=1)
        return carry

    lax.fori_loop(0, n_col, attend_back, 0)
    pair_buf[0] = d_key_buf[held : 2 * held, :].astype(jnp.bfloat16)
    pair_buf[1] = d_value_buf[held : 2 * held, :].astype(jnp.bfloat16)
    crossing = put(pair_buf, away_buf, pair_sends.at[0], pair_recvs.at[0], "row", partner)
    crossing.start()
    gq_buf[...] = mix(normed_ref[...], d_query_buf[...], 0, 0).astype(jnp.bfloat16)
    go_buf[...] = mix(d_branch_ref[...], att_ref[...], 0, 0).astype(jnp.bfloat16)
    crossing.wait_recv()
    d_key = d_key_buf[0:held, :] + away_buf[0].astype(jnp.float32)
    d_value = d_value_buf[0:held, :] + away_buf[1].astype(jnp.float32)
    d_pair_buf[...] = jnp.concatenate([d_key, d_value], axis=1).astype(jnp.bfloat16)
    sums = Reduce("col", n_col, sum_out, sum_in, sends, recvs, 0)

    def spread(step, carry):
        owner = ring(col_at, step, n_col)
        partial = mix(d_query_buf[span(owner, slot), :], wq_ref[...], 1, 1) + mix(
            d_pair_buf[span(owner, slot), :], wkv_ref[...], 1, 1
        )

        @pl.when(step < n_col)
        def _():
            sums.send(step, partial)

        @pl.when(step == n_col)
        def _():
            own_sum[...] = partial

        return carry

    lax.fori_loop(1, n_col + 1, spread, 0)
    gkv_buf[...] = mix(normed_ref[...], d_pair_buf[...], 0, 0).astype(jnp.bfloat16)
    early = [
        Scatter("row", n_row, gq_buf, gq_in, sends, recvs, 6),
        Scatter("row", n_row, gkv_buf, gkv_in, sends, recvs, 7),
        Scatter("row", n_row, go_buf, go_in, sends, recvs, 8),
    ]
    for scatter in early:
        scatter.start()
    late_shares = [
        Share("dp", n_dp, g1_own, g1_dp, sends, recvs, 9),
        Share("dp", n_dp, g2_own, g2_dp, sends, recvs, 10),
    ]
    for scatter, share in zip(late, late_shares):
        share.begin(scatter.total())
    own_block[...] = (
        resid_ref[...] + lasts.total(own_last[...]) + vec_ref[5:6, :]
    ).astype(jnp.bfloat16)
    blocks = Gather("row", n_row, own_block, block_buf, sends, recvs, 4)
    blocks.start()
    blocks.keep_own()
    query_sums = column_sums(d_query_buf[...].astype(jnp.float32))
    pair_sums = column_sums(d_pair_buf[...].astype(jnp.float32))
    scaled, inv_std = norm_stats(x_ref[...].astype(jnp.float32))
    d_normed = sums.total(own_sum[...])
    own_frames[...] = (
        d_resid_ref[...] + norm_backward(d_normed, scaled, inv_std, vec_ref[0:1, :])
    ).astype(jnp.bfloat16)
    wholes = Gather("row", n_row, own_frames, frames_buf, sends, recvs, 5)
    wholes.start()
    wholes.keep_own()
    features = Share("col", n_col, feature_own, feature_buf, sends, recvs, 14)
    features.begin(
        jnp.concatenate(
            [
                column_sums(d_normed * scaled),
                column_sums(d_normed),
                small_two_ref[...],
                jnp.zeros((2, width), jnp.float32),
            ],
            axis=0,
        )
    )
    early_shares = [
        Share("dp", n_dp, gq_own, gq_dp, sends, recvs, 11),
        Share("dp", n_dp, gkv_own, gkv_dp, sends, recvs, 12),
        Share("dp", n_dp, go_own, go_dp, sends, recvs, 13),
    ]
    for scatter, share in zip(early, early_shares):
        share.begin(scatter.total())
    heads = jnp.concatenate(
        [query_sums, pair_sums, jnp.zeros((1, width - 3 * head_width), jnp.float32)], axis=1
    )
    smalls = Share("row", n_row, small_own, small_buf, sends, recvs, 15)
    smalls.begin(
        jnp.concatenate(
            [
                features.total(),
                hidden_sum_ref[...],
                heads,
                jnp.zeros((6, width), jnp.float32),
            ],
            axis=0,
        )
    )
    finals = Share("dp", n_dp, last_own, last_buf, sends, recvs, 16)
    finals.begin(smalls.total())
    g1_out[...] = late_shares[0].total()
    g2_out[...] = late_shares[1].total()
    gq_out[...] = early_shares[0].total()
    gkv_out[...] = early_shares[1].total()
    go_out[...] = early_shares[2].total()
    blocks.wait()
    block_out[...] = block_buf[...]
    wholes.wait()
    frames_out[...] = frames_buf[...]
    summed = finals.total()
    feature_out[...] = summed[0:8]
    head_out[...] = summed[8:16]
    crossing.wait_send()
    for sent in [sums, lasts, blocks, wholes, features, smalls, finals]:
        sent.finish()
    for sent in late + early + late_shares + early_shares:
        sent.finish()


def call(kernel, name, number, flops, outs, scratch, *operands):
    return pl.pallas_call(
        kernel,
        in_specs=[pl.BlockSpec(memory_space=pltpu.VMEM)] * len(operands),
        out_specs=[pl.BlockSpec(memory_space=pltpu.VMEM)] * len(outs),
        out_shape=[jax.ShapeDtypeStruct(shape, kind) for shape, kind in outs],
        scratch_shapes=scratch,
        compiler_params=pltpu.CompilerParams(
            vmem_limit_bytes=VMEM_LIMIT, collective_id=number, has_side_effects=True
        ),
        cost_estimate=pl.CostEstimate(flops=flops, bytes_accessed=60000000, transcendentals=0),
        name=name,
    )(*operands)


def local(
    frames,
    ln1_gain,
    ln1_bias,
    w_query,
    b_query,
    w_key,
    w_value,
    b_value,
    w_out,
    b_out,
    ln2_gain,
    ln2_bias,
    w_fc1,
    b_fc1,
    w_fc2,
    b_fc2,
    cotangent,
):
    row_count = lax.axis_size("row")
    col_count = lax.axis_size("col")
    row_at = lax.axis_index("row")
    col_at = lax.axis_index("col")
    head_width = w_query.shape[1]
    hidden_part = w_fc1.shape[1]
    clip_count, frame_count, width = frames.shape
    feature_part = width // row_count
    parts = row_count // clip_count
    slot = -(-frame_count // (parts * 64)) * 64
    padding = ((0, 0), (0, slot * parts - frame_count), (0, 0))
    clip_at = row_at // parts
    part_at = row_at % parts

    def own_frames(tensor):
        piece = lax.dynamic_slice(
            jnp.pad(tensor, padding), (clip_at, part_at * slot, 0), (1, slot, width)
        )
        return piece[0]

    def part_mask(part):
        real = part * slot + jnp.arange(slot) < frame_count
        return jnp.tile(jnp.where(real, 0.0, -1e30).astype(jnp.float32), col_count)

    bf16, f32 = jnp.bfloat16, jnp.float32
    held = slot * col_count
    away = max(row_count, col_count, lax.axis_size("dp")) - 1
    dma = pltpu.SemaphoreType.DMA
    late = gather_rows(jnp.concatenate([w_fc1, w_fc2], axis=1))
    bias_query = take_piece(b_query, col_at, head_width)
    bias_value = take_piece(b_value, col_at, head_width)
    bias_hidden = take_piece(b_fc1, col_at, hidden_part)
    bias_pair = jnp.concatenate([jnp.zeros_like(bias_value), bias_value])
    stacked = jnp.stack(
        [ln1_gain, ln1_bias, ln2_gain, ln2_bias, b_out, b_fc2, jnp.zeros_like(b_out), jnp.zeros_like(b_out)]
    )
    vec_part = lax.dynamic_update_slice(
        jnp.zeros((8, width), f32), stacked, (0, row_at * feature_part)
    )
    inputs_own = own_frames(frames)
    cotangent_part = own_frames(cotangent)
    dp_count = lax.axis_size("dp")
    mask = jnp.concatenate([part_mask((part_at - shift) % parts) for shift in range(parts)])[None]
    block = pltpu.VMEM((slot, width), bf16)
    total = pltpu.VMEM((slot, width), f32)
    blocks = pltpu.VMEM((col_count - 1, slot, width), bf16)
    (
        vectors, wq, wkv, wo, normed_all, query_part, pair_whole, attended, log_total, residual,
        normed_two, cotangent_all,
    ) = call(
        functools.partial(front_kernel, row_count, col_count), "front", 1, 4 * 10**10,
        [
            ((8, width), f32), ((width, head_width), bf16), ((width, 2 * head_width), bf16),
            ((width, head_width), bf16), ((held, width), bf16), ((held, head_width), bf16),
            ((parts * held, 2 * head_width), bf16), ((held, head_width), bf16),
            ((held, head_width // HEAD), f32), ((slot, width), f32), ((slot, width), bf16),
            ((held, width), bf16),
        ],
        [
            pltpu.VMEM((held, width), bf16),
            pltpu.VMEM((row_count - 1, 8, width), f32),
            pltpu.VMEM((width, head_width), bf16),
            pltpu.VMEM((width, 2 * head_width), bf16),
            pltpu.VMEM((width, head_width), bf16),
            block,
            pltpu.VMEM((held, width), bf16),
            pltpu.VMEM((held, 2 * head_width), bf16),
            pltpu.VMEM((held, 2 * head_width), bf16),
            blocks, blocks, total,
            dma((7, away)), dma((7, away)), dma((col_count,)), dma((col_count,)),
        ],
        inputs_own, cotangent_part, vec_part, w_query, jnp.concatenate([w_key, w_value], axis=1), w_out.T,
        bias_query[None], bias_pair[None], mask,
    )
    hidden_all, d_branch_all, d_residual, grad_first, grad_second, small_two, hidden_sums = call(
        functools.partial(middle_kernel, col_count), "middle", 2, 4 * 10**10,
        [
            ((held, hidden_part), bf16), ((held, width), bf16), ((slot, width), f32),
            ((width, hidden_part), bf16), ((width, hidden_part), bf16), ((4, width), f32),
            ((1, hidden_part), f32),
        ],
        [
            pltpu.VMEM((held, width), bf16),
            pltpu.VMEM((held, hidden_part), bf16),
            block,
            pltpu.VMEM((held, width), bf16),
            blocks, blocks, total,
            dma((4, away)), dma((4, away)),
        ],
        normed_two, residual, cotangent_part, cotangent_all, late[:, :hidden_part],
        late[:, hidden_part:], vectors, bias_hidden[None],
    )
    head = (feature_part, head_width)
    pair = (feature_part, 2 * head_width)
    hide = (feature_part, hidden_part)

    def several(count, *shapes):
        return [pltpu.VMEM((count,) + shape, bf16) for shape in shapes]

    def stacks(count, *shapes):
        return [pltpu.VMEM((count * shape[0], shape[1]), bf16) for shape in shapes]

    block_all, grad_all, features, heads, grad_1, grad_2, grad_q, grad_kv, grad_o = call(
        functools.partial(back_kernel, dp_count, row_count, col_count), "back", 3, 4 * 10**10,
        [
            ((row_count * slot, width), bf16), ((row_count * slot, width), bf16),
            ((8, width), f32), ((8, width), f32),
            (hide, f32), (hide, f32), (head, f32), (pair, f32), (head, f32),
        ],
        [
            pltpu.VMEM((held, head_width), bf16),
            pltpu.VMEM((parts * held, head_width), f32),
            pltpu.VMEM((parts * held, head_width), f32),
            pltpu.VMEM((2, held, head_width), bf16),
            pltpu.VMEM((2, held, head_width), bf16),
            pltpu.VMEM((held, 2 * head_width), bf16),
            blocks, blocks, total, blocks, blocks, total,
            block, pltpu.VMEM((row_count * slot, width), bf16),
            block, pltpu.VMEM((row_count * slot, width), bf16),
        ]
        + stacks(row_count, head, pair, head)
        + several(row_count - 1, hide, hide, head, pair, head)
        + stacks(1, hide, hide, head, pair, head)
        + stacks(dp_count, hide, hide, head, pair, head)
        + [
            pltpu.VMEM((8, width), f32), pltpu.VMEM((col_count * 8, width), f32),
            pltpu.VMEM((16, width), f32), pltpu.VMEM((row_count * 16, width), f32),
            pltpu.VMEM((16, width), f32), pltpu.VMEM((dp_count * 16, width), f32),
            dma((17, away)), dma((17, away)), dma((1,)), dma((1,)),
        ],
        inputs_own, d_residual, vectors, wq, wkv, wo, normed_all, query_part, pair_whole, attended,
        log_total, mask, d_branch_all, hidden_all, late[:, hidden_part:], residual, grad_first,
        grad_second, small_two, hidden_sums,
    )
    featured_sums = lax.dynamic_slice(
        features, (0, row_at * feature_part), (features.shape[0], feature_part)
    )

    def whole_frames(whole):
        return whole.reshape(clip_count, parts * slot, width)[:, :frame_count]

    return (
        whole_frames(block_all),
        whole_frames(grad_all),
        featured_sums[0],
        featured_sums[1],
        grad_q,
        heads[1, :head_width],
        grad_kv[:, :head_width],
        grad_kv[:, head_width:],
        heads[1, 2 * head_width : 3 * head_width],
        grad_o.T,
        featured_sums[4],
        featured_sums[2],
        featured_sums[3],
        grad_1,
        heads[0],
        grad_2,
        featured_sums[5],
    )


def solution(mesh):
    placed = (
        P("dp", "col", None),
        P("row"),
        P("row"),
        P("row", "col"),
        P(),
        P("row", "col"),
        P("row", "col"),
        P(),
        P("col", "row"),
        P("row"),
        P("row"),
        P("row"),
        P("row", "col"),
        P(),
        P("row", "col"),
        P("row"),
        P("dp", "col", None),
    )
    return jax.shard_map(
        local,
        mesh=mesh,
        in_specs=placed,
        out_specs=(
            P("dp", "col", None),
            P("dp", "col", None),
            P("row"),
            P("row"),
            P("row", "col"),
            P("col"),
            P("row", "col"),
            P("row", "col"),
            P("col"),
            P("col", "row"),
            P("row"),
            P("row"),
            P("row"),
            P("row", "col"),
            P("col"),
            P("row", "col"),
            P("row"),
        ),
        check_vma=False,
    )
```
